256 devices in a mesh: chan: 16 (over x, y_hi, core), win: 16 (over y_lo, z).
Axes of the slice: x: 4, y: 4 (y_hi: 2, y_lo: 2; y = y_hi * 2 + y_lo), z: 8, core: 2. Of those that a mesh axis runs over, the one named last changes fastest.
Arguments:
- signals: bfloat16 [16, 1024, 2048], P('win', 'chan'), may hold values from -1024 to 1024
- plan: int32 [4], replicated, may hold values from 1 to 15, as said below
- lag_half: int32 [4, 16], replicated, may hold values from 0 to 1, as said below
Outputs:
- xcorr: float32 [4, 1024, 2112], P(None, 'chan', 'win')
The draws below stay inside these ranges and needn't reach their ends.
Inputs may be any that keep to these rules, and one draw needn't show every extreme that they name: The entries are distinct, so block b meets block b XOR plan[m] in matching m; 1 and 15 are among them. `lag_half`: the two blocks of a pair carry equal entries.
All inputs are finite; a program needn't handle non-finite values.
Results may differ from the reference program's by a relative error of at most 0.006.
Values may be sent and summed in bfloat16 or wider, within the bound.
No kernel may reach another device: no remote copies, remote signals or barrier semaphores. Data moves between devices by JAX's collectives and lax.ppermute only.
A program may use at most 64 MiB of HBM per device.

```python
import math
import jax
import jax.numpy as jnp
from jax import lax

CH_BLK = 64
NT = 2048
BAND = 128
LAGS = 33
MATCH = 4
NBLK = 16
CHANNELS = 1024
WINDOWS = 16


def masks_of(key):
    inner = jax.random.fold_in(key, 11)
    middle = jax.random.permutation(inner, NBLK - 3).astype(jnp.int32) + 2
    picked = jnp.concatenate([jnp.array([1, NBLK - 1], dtype=jnp.int32), middle[:MATCH - 2]])
    order = jax.random.permutation(jax.random.fold_in(inner, 5), MATCH)
    return picked[order]


def draw_plan(key, part):
    return masks_of(key)


def draw_lag_half(key, part):
    pair_masks = masks_of(key)
    key = jax.random.fold_in(key, 7)
    coins = jax.random.randint(key, (MATCH, NBLK), 0, 2).astype(jnp.int32)
    labels = jnp.arange(NBLK, dtype=jnp.int32)
    lower = jnp.minimum(labels[None, :], labels[None, :] ^ pair_masks[:, None])
    return jnp.take_along_axis(coins, lower, axis=1)


def draw_signals(key, part):
    key = jax.random.fold_in(key, 3)
    first, second, third = jax.random.split(key, 3)
    noise = jax.random.truncated_normal(first, -4.0, 4.0, (WINDOWS, CHANNELS, NT), jnp.float32)
    top = 10.0
    channel_scale = jnp.exp(jax.random.uniform(second, (WINDOWS, CHANNELS, 1), jnp.float32, 0.0, math.log(top)))
    envelope = jnp.exp(jax.random.uniform(third, (WINDOWS, 1, NT // 64), jnp.float32, 0.0, math.log(top)))
    envelope = jnp.repeat(envelope, 64, axis=2)
    return (noise * channel_scale * envelope).astype(jnp.bfloat16)


def setup_inputs(seed: int = 0) -> dict:
    key_of = jax.random.split(jax.random.key(seed), 4)
    signals = draw_signals(jax.random.fold_in(key_of[3], 71), 0)
    plan = draw_plan(jax.random.fold_in(key_of[3], 71), 0)
    lag_half = draw_lag_half(jax.random.fold_in(key_of[3], 71), 0)
    return {"signals": signals, "plan": plan, "lag_half": lag_half}


def dft_table(samples):
    bins = samples // 2
    times = jnp.arange(samples, dtype=jnp.int32)
    freqs = jnp.arange(bins, dtype=jnp.int32)
    phase = times[:, None] * freqs[None, :] % samples
    angle = phase.astype(jnp.float32) * (2.0 * math.pi / samples)
    return jnp.concatenate([jnp.cos(angle), jnp.sin(angle)], axis=1).astype(jnp.bfloat16)

def whiten(signals, transform):
    windows_here, block_width, samples = signals.shape
    bins = samples // 2
    spectrum = jnp.einsum('wct,tf->wcf', signals.astype(jnp.float32), transform.astype(jnp.float32))
    real_bands = spectrum[:, :, :bins].reshape(windows_here, block_width, bins // BAND, BAND)
    sine_bands = spectrum[:, :, bins:].reshape(windows_here, block_width, bins // BAND, BAND)
    energy = lax.optimization_barrier(jnp.mean(real_bands * real_bands + sine_bands * sine_bands, axis=3, keepdims=True))
    factor = lax.rsqrt(energy + 1e-06)
    whitened = jnp.concatenate([(real_bands * factor).reshape(windows_here, block_width, bins), (sine_bands * factor).reshape(windows_here, block_width, bins)], axis=2).astype(jnp.bfloat16)
    series = jnp.einsum('wcf,tf->wct', whitened.astype(jnp.float32), transform.astype(jnp.float32)) * bins ** (-0.5)
    return series.astype(jnp.bfloat16)

def reference(signals, plan, lag_half):
    transform = dft_table(NT)
    series = whiten(signals, transform).astype(jnp.float32)
    block_count = CHANNELS // CH_BLK
    blocks = series.reshape(WINDOWS, block_count, CH_BLK, NT)
    labels = jnp.arange(block_count, dtype=jnp.int32)

    def one_matching(matching):
        pair_mask = plan[matching]
        partner = jnp.take(blocks, labels ^ pair_mask, axis=1)
        forward = lag_half[matching] == 0

        def one_lag(offset):
            amounts = jnp.where(forward, -offset, offset).astype(jnp.int32)
            moved = jax.vmap(lambda segment, amount: jnp.roll(segment, amount, axis=-1), in_axes=(1, 0), out_axes=1)(partner, amounts)
            return jnp.einsum('wbit,wbjt->bij', blocks, moved)
        lagged = lax.map(one_lag, jnp.arange(LAGS, dtype=jnp.int32))
        return jnp.transpose(lagged, (1, 2, 3, 0)).reshape(CHANNELS, CH_BLK * LAGS)
    stacked = lax.map(one_matching, jnp.arange(MATCH, dtype=jnp.int32))
    return stacked * (1.0 / math.sqrt(WINDOWS * NT))
```

```python
import functools
import math

import jax
import jax.numpy as jnp
import numpy as np
from jax import lax
from jax.experimental import pallas as pl
from jax.experimental.pallas import tpu as pltpu
from jax.sharding import PartitionSpec as P

BAND = 128
LAGS = 33
MATCH = 4
NT = 2048
BINS = NT // 2
QUART = NT // 4
CH = 64
FINE = 4
COARSE = 8
VMEM = 48 * 1024 * 1024


def quarter_table():
    times = np.arange(QUART, dtype=np.int64)
    freqs = np.arange(BINS, dtype=np.int64)
    angle = (times[:, None] * freqs[None, :] % NT) * (2.0 * math.pi / NT)
    return np.concatenate([np.cos(angle), np.sin(angle)], axis=1).astype(np.float32).astype(jnp.bfloat16)


def pairs():
    return [(a, b) for a in range(2, 15) for b in range(a + 1, 15)]


def scalars_kernel(plan_ref, half_ref, own_ref, info_ref):
    own = own_ref[0]
    masks = [plan_ref[m] for m in range(MATCH)]
    high = jnp.int32(0)
    low = jnp.int32(99)
    for mask in masks:
        other = jnp.logical_and(mask != 1, mask != 15)
        low = jnp.where(other, jnp.minimum(low, mask), low)
        high = jnp.where(other, jnp.maximum(high, mask), high)
    info_ref[0] = 14 * (low - 2) - (low * (low - 1)) // 2 + 1 + high - low - 1
    for slot, wanted in enumerate((jnp.int32(1), jnp.int32(15), low, high)):
        place = jnp.int32(0)
        for m in range(MATCH):
            place = jnp.where(masks[m] == wanted, m, place)
        info_ref[1 + slot] = place
        info_ref[5 + slot] = 1 - 2 * half_ref[place, own]


def scalars(plan, lag_half, own):
    smem = pl.BlockSpec(memory_space=pltpu.SMEM)
    return pl.pallas_call(
        scalars_kernel,
        out_shape=jax.ShapeDtypeStruct((16,), jnp.int32),
        in_specs=[smem, smem, smem],
        out_specs=smem,
    )(plan, lag_half, own)


def rolled(value, shift):
    shift %= value.shape[1]
    if shift == 0:
        return value
    cut = value.shape[1] - shift
    return jnp.concatenate([value[:, cut:], value[:, :cut]], axis=1)


def whiten_kernel(x_ref, table_ref, series_ref, fine_ref):
    stacked = jnp.concatenate([x_ref[:, r * QUART : (r + 1) * QUART] for r in range(4)], axis=0)
    spectrum = jnp.dot(stacked, table_ref[...], preferred_element_type=jnp.float32)
    residue = lax.broadcasted_iota(jnp.int32, (CH, BAND), 1) % 4
    even = residue % 2 == 0
    alternate = jnp.where(even, 1.0, -1.0)
    halfturn = jnp.where(residue < 2, 1.0, -1.0)
    reals, sines = [], []
    for band in range(BINS // BAND):
        cos = [spectrum[r * CH : (r + 1) * CH, band * BAND : (band + 1) * BAND] for r in range(4)]
        sin = [
            spectrum[r * CH : (r + 1) * CH, BINS + band * BAND : BINS + (band + 1) * BAND]
            for r in range(4)
        ]
        real = cos[0] + alternate * cos[2] + halfturn * jnp.where(even, cos[1] + cos[3], sin[3] - sin[1])
        sine = sin[0] + alternate * sin[2] + halfturn * jnp.where(even, sin[1] + sin[3], cos[1] - cos[3])
        energy = jnp.mean(real * real + sine * sine, axis=1, keepdims=True)
        factor = lax.rsqrt(energy + 1e-06)
        reals.append((real * factor).astype(jnp.bfloat16).astype(jnp.float32))
        sines.append((sine * factor).astype(jnp.bfloat16).astype(jnp.float32))
    rows = []
    for r in range(4):
        cos_part, sin_part = [], []
        for real, sine in zip(reals, sines):
            if r == 0:
                u, v = real, sine
            elif r == 2:
                u, v = alternate * real, alternate * sine
            else:
                turn = halfturn if r == 1 else halfturn * alternate
                u = turn * jnp.where(even, real, sine)
                v = turn * jnp.where(even, sine, -real)
            cos_part.append(u.astype(jnp.bfloat16))
            sin_part.append(v.astype(jnp.bfloat16))
        rows.append(jnp.concatenate(cos_part + sin_part, axis=1))
    turned = jnp.concatenate(rows, axis=0)
    out = lax.dot_general(
        turned, table_ref[...], (((1,), (1,)), ((), ())), preferred_element_type=jnp.float32
    ) * BINS ** (-0.5)
    series = jnp.concatenate(
        [out[r * CH : (r + 1) * CH] for r in range(4)], axis=1
    ).astype(jnp.bfloat16)
    series_ref[...] = series
    for fine in range(FINE):
        fine_ref[fine * CH : (fine + 1) * CH, :] = rolled(series, fine)


def whiten(signals, table):
    return pl.pallas_call(
        whiten_kernel,
        out_shape=[
            jax.ShapeDtypeStruct((CH, NT), jnp.bfloat16),
            jax.ShapeDtypeStruct((FINE * CH, NT), jnp.bfloat16),
        ],
        compiler_params=pltpu.CompilerParams(vmem_limit_bytes=VMEM),
    )(signals, table)


def correlate_kernel(info_ref, fine_ref, partner_ref, out_ref, coarse, *, slot):
    partner = partner_ref[...]
    partner = jnp.where(info_ref[5 + slot] > 0, partner, rolled(partner, LAGS - 1))
    for step in range(COARSE + 1):
        coarse[step * CH : (step + 1) * CH, :] = rolled(partner, -FINE * step)
    dims = (((1,), (1,)), ((), ()))
    main = lax.dot_general(
        coarse[: COARSE * CH, :], fine_ref[...], dims, preferred_element_type=jnp.float32
    )
    last = lax.dot_general(
        coarse[COARSE * CH :, :], fine_ref[:CH, :], dims, preferred_element_type=jnp.float32
    )
    for part in range(16):
        for step in range(COARSE):
            out_ref[part, step * 4 : step * 4 + 4, :] = main[step * CH + part * 4 : step * CH + part * 4 + 4, :]
        for one in range(4):
            out_ref[part, 32:33, one * CH : (one + 1) * CH] = last[part * 4 + one : part * 4 + one + 1, :]


def correlate(info, fine, partner, slot):
    vmem = pl.BlockSpec(memory_space=pltpu.VMEM)
    return pl.pallas_call(
        functools.partial(correlate_kernel, slot=slot),
        out_shape=jax.ShapeDtypeStruct((16, LAGS, FINE * CH), jnp.float32),
        in_specs=[pl.BlockSpec(memory_space=pltpu.SMEM), vmem, vmem],
        out_specs=vmem,
        scratch_shapes=[pltpu.VMEM(((COARSE + 1) * CH, NT), jnp.bfloat16)],
        compiler_params=pltpu.CompilerParams(vmem_limit_bytes=VMEM),
        cost_estimate=pl.CostEstimate(flops=2 * CH * CH * LAGS * NT, bytes_accessed=4 << 20, transcendentals=0),
    )(info, fine, partner)


def finish_kernel(info_ref, sums_ref, out_ref, *, factor):
    slot = pl.program_id(0)
    backward = info_ref[5 + slot] < 0
    columns = lax.broadcasted_iota(jnp.int32, (LAGS, 4 * LAGS), 1)
    rows = lax.broadcasted_iota(jnp.int32, (LAGS, 4 * LAGS), 0)
    sums = sums_ref[0]
    total = jnp.zeros((CH, 4 * LAGS), jnp.float32)
    for fine in range(FINE):
        lag = (rows // 4) * FINE + fine
        one = rows % 4
        lag = jnp.where(backward, LAGS - 1 - lag, lag)
        pick = jnp.logical_and(columns == one * LAGS + lag, rows < 32)
        last = jnp.where(backward, 0, LAGS - 1)
        pick = jnp.logical_or(pick, jnp.logical_and(rows == 32, columns == fine * LAGS + last))
        total += lax.dot_general(
            sums[:, fine * CH : (fine + 1) * CH],
            jnp.where(pick, factor, 0.0),
            (((0,), (0,)), ((), ())),
            precision=lax.Precision.HIGHEST,
            preferred_element_type=jnp.float32,
        )
    out_ref[0] = total


def finish(info, sums, factor):
    return pl.pallas_call(
        functools.partial(finish_kernel, factor=factor),
        out_shape=jax.ShapeDtypeStruct((MATCH, CH, 4 * LAGS), jnp.float32),
        grid_spec=pltpu.PrefetchScalarGridSpec(
            num_scalar_prefetch=1,
            grid=(MATCH,),
            in_specs=[pl.BlockSpec((1, LAGS, FINE * CH), lambda slot, info: (slot, 0, 0))],
            out_specs=pl.BlockSpec((1, CH, 4 * LAGS), lambda slot, info: (info[1 + slot], 0, 0)),
        ),
    )(info, sums)


def exchange(series, mask):
    return lax.ppermute(series, "chan", [(block, block ^ mask) for block in range(16)])


def shards(signals, plan, lag_half):
    table = jnp.asarray(quarter_table())
    own = lax.axis_index("chan").astype(jnp.int32).reshape(1)
    info = scalars(plan, lag_half, own)
    series, fine = whiten(signals[0], table)
    near = exchange(series, 1)
    far = exchange(series, 15)
    low, high = lax.switch(
        info[0],
        [lambda s, a=a, b=b: (exchange(s, a), exchange(s, b)) for a, b in pairs()],
        series,
    )
    terms = [correlate(info, fine, partner, slot) for slot, partner in enumerate((near, far, low, high))]
    stacked = jnp.stack(terms, axis=1)
    sums = lax.psum_scatter(
        stacked.reshape(16 * MATCH * LAGS, FINE * CH), "win", scatter_dimension=0, tiled=True
    )
    factor = 1.0 / math.sqrt(lax.axis_size("win") * NT)
    return finish(info, sums.reshape(MATCH, LAGS, FINE * CH), factor)


def solution(mesh):
    placed = (P("win", "chan", None), P(), P())
    return jax.shard_map(
        shards, mesh=mesh, in_specs=placed, out_specs=P(None, "chan", "win"), check_vma=False
    )
```

```python
import functools
import math

import jax
import jax.numpy as jnp
import numpy as np
from jax import lax
from jax.experimental import pallas as pl
from jax.experimental.pallas import tpu as pltpu
from jax.sharding import PartitionSpec as P

BAND = 128
LAGS = 33
MATCH = 4
NT = 2048
BINS = NT // 2
QUART = NT // 4
CH = 64
FINE = 4
COARSE = 8
VMEM = 48 * 1024 * 1024


def quarter_table():
    times = np.arange(QUART, dtype=np.int64)
    freqs = np.arange(BINS, dtype=np.int64)
    angle = (times[:, None] * freqs[None, :] % NT) * (2.0 * math.pi / NT)
    return np.concatenate([np.cos(angle), np.sin(angle)], axis=1).astype(np.float32).astype(jnp.bfloat16)


def scalars_kernel(plan_ref, half_ref, own_ref, info_ref):
    own = own_ref[0]
    window = own_ref[1]
    masks = [plan_ref[m] for m in range(MATCH)]
    high = jnp.int32(0)
    low = jnp.int32(99)
    for mask in masks:
        other = jnp.logical_and(mask != 1, mask != 15)
        low = jnp.where(other, jnp.minimum(low, mask), low)
        high = jnp.where(other, jnp.maximum(high, mask), high)
    info_ref[0] = low
    info_ref[9] = high
    for slot, wanted in enumerate((jnp.int32(1), jnp.int32(15), low, high)):
        place = jnp.int32(0)
        for m in range(MATCH):
            place = jnp.where(masks[m] == wanted, m, place)
        info_ref[1 + slot] = place
        info_ref[5 + slot] = 1 - 2 * half_ref[place, own]
    info_ref[10] = (window >> 3) * 2 + (window & 1)
    info_ref[11] = (window >> 1) & 3


def scalars(plan, lag_half, own):
    smem = pl.BlockSpec(memory_space=pltpu.SMEM)
    return pl.pallas_call(
        scalars_kernel,
        out_shape=jax.ShapeDtypeStruct((16,), jnp.int32),
        in_specs=[smem, smem, smem],
        out_specs=smem,
    )(plan, lag_half, own)


def rolled(value, shift):
    shift %= value.shape[1]
    if shift == 0:
        return value
    cut = value.shape[1] - shift
    return jnp.concatenate([value[:, cut:], value[:, :cut]], axis=1)


def whiten_kernel(x_ref, table_ref, series_ref, fine_ref):
    stacked = jnp.concatenate([x_ref[:, r * QUART : (r + 1) * QUART] for r in range(4)], axis=0)
    spectrum = jnp.dot(stacked, table_ref[...], preferred_element_type=jnp.float32)
    residue = lax.broadcasted_iota(jnp.int32, (CH, BAND), 1) % 4
    even = residue % 2 == 0
    alternate = jnp.where(even, 1.0, -1.0)
    halfturn = jnp.where(residue < 2, 1.0, -1.0)
    reals, sines = [], []
    for band in range(BINS // BAND):
        cos = [spectrum[r * CH : (r + 1) * CH, band * BAND : (band + 1) * BAND] for r in range(4)]
        sin = [
            spectrum[r * CH : (r + 1) * CH, BINS + band * BAND : BINS + (band + 1) * BAND]
            for r in range(4)
        ]
        real = cos[0] + alternate * cos[2] + halfturn * jnp.where(even, cos[1] + cos[3], sin[3] - sin[1])
        sine = sin[0] + alternate * sin[2] + halfturn * jnp.where(even, sin[1] + sin[3], cos[1] - cos[3])
        energy = jnp.mean(real * real + sine * sine, axis=1, keepdims=True)
        factor = lax.rsqrt(energy + 1e-06)
        reals.append((real * factor).astype(jnp.bfloat16).astype(jnp.float32))
        sines.append((sine * factor).astype(jnp.bfloat16).astype(jnp.float32))
    rows = []
    for r in range(4):
        cos_part, sin_part = [], []
        for real, sine in zip(reals, sines):
            if r == 0:
                u, v = real, sine
            elif r == 2:
                u, v = alternate * real, alternate * sine
            else:
                turn = halfturn if r == 1 else halfturn * alternate
                u = turn * jnp.where(even, real, sine)
                v = turn * jnp.where(even, sine, -real)
            cos_part.append(u.astype(jnp.bfloat16))
            sin_part.append(v.astype(jnp.bfloat16))
        rows.append(jnp.concatenate(cos_part + sin_part, axis=1))
    turned = jnp.concatenate(rows, axis=0)
    out = lax.dot_general(
        turned, table_ref[...], (((1,), (1,)), ((), ())), preferred_element_type=jnp.float32
    ) * BINS ** (-0.5)
    series = jnp.concatenate(
        [out[r * CH : (r + 1) * CH] for r in range(4)], axis=1
    ).astype(jnp.bfloat16)
    series_ref[...] = series
    for fine in range(FINE):
        fine_ref[fine * CH : (fine + 1) * CH, :] = rolled(series, fine)


def whiten(signals, table):
    return pl.pallas_call(
        whiten_kernel,
        out_shape=[
            jax.ShapeDtypeStruct((CH, NT), jnp.bfloat16),
            jax.ShapeDtypeStruct((FINE * CH, NT), jnp.bfloat16),
        ],
        compiler_params=pltpu.CompilerParams(vmem_limit_bytes=VMEM),
    )(signals, table)


def correlate_kernel(info_ref, fine_ref, first_ref, second_ref, out_ref, coarse, sums, lasts, *, batch):
    dims = (((1,), (1,)), ((), ()))
    for pair, partner_ref in enumerate((first_ref, second_ref)):
        partner = partner_ref[...]
        partner = jnp.where(info_ref[5 + 2 * batch + pair] > 0, partner, rolled(partner, LAGS - 1))
        for step in range(COARSE + 1):
            coarse[step * CH : (step + 1) * CH, :] = rolled(partner, -FINE * step)
        main = lax.dot_general(
            coarse[: COARSE * CH, :], fine_ref[...], dims, preferred_element_type=jnp.float32
        )
        last = lax.dot_general(
            coarse[COARSE * CH :, :], fine_ref[:CH, :], dims, preferred_element_type=jnp.float32
        )
        for q in range(16):
            for step in range(COARSE):
                row = step * CH + q * 4
                sums[q, step * 4 : step * 4 + 4, :] = main[row : row + 4, :]
            group = (q >> 3) * 2 + (q & 1)
            spot = ((q >> 1) & 3) * 2 + pair
            for one in range(4):
                lasts[group, spot : spot + 1, one * CH : (one + 1) * CH] = last[q * 4 + one : q * 4 + one + 1, :]
        for q in range(16):
            group = (q >> 3) * 2 + (q & 1)
            row = ((q >> 1) & 3) * 64 + pair * 32
            out_ref[group ^ info_ref[10], row : row + 32, :] = sums[q].astype(jnp.bfloat16)
    for group in range(4):
        out_ref[group ^ info_ref[10], 256:272, :] = lasts[group].astype(jnp.bfloat16)


def correlate(info, fine, first, second, batch):
    vmem = pl.BlockSpec(memory_space=pltpu.VMEM)
    return pl.pallas_call(
        functools.partial(correlate_kernel, batch=batch),
        out_shape=jax.ShapeDtypeStruct((4, 272, FINE * CH), jnp.bfloat16),
        in_specs=[pl.BlockSpec(memory_space=pltpu.SMEM), vmem, vmem, vmem],
        out_specs=vmem,
        scratch_shapes=[
            pltpu.VMEM(((COARSE + 1) * CH, NT), jnp.bfloat16),
            pltpu.VMEM((16, 32, FINE * CH), jnp.float32),
            pltpu.VMEM((4, 16, FINE * CH), jnp.float32),
        ],
        compiler_params=pltpu.CompilerParams(vmem_limit_bytes=VMEM),
        cost_estimate=pl.CostEstimate(flops=4 * CH * CH * LAGS * NT, bytes_accessed=4 << 20, transcendentals=0),
    )(info, fine, first, second)


def gather_kernel(info_ref, *refs):
    out_ref, lasts = refs[8:]
    for batch in range(2):
        own_ref, *others = refs[batch * 4 : batch * 4 + 4]
        for zz in range(4):
            rows = slice(zz * 64, zz * 64 + 64)
            total = own_ref[0, rows, :].astype(jnp.float32)
            for other in others:
                total += other[rows, :].astype(jnp.float32)
            out_ref[zz ^ info_ref[11], batch * 64 : batch * 64 + 64, :] = total.astype(jnp.bfloat16)
        total = own_ref[0, 256:272, :].astype(jnp.float32)
        for other in others:
            total += other[256:272, :].astype(jnp.float32)
        for zz in range(4):
            lasts[zz, batch * 2 : batch * 2 + 2, :] = total[zz * 2 : zz * 2 + 2, :]
    for zz in range(4):
        out_ref[zz ^ info_ref[11], 128:144, :] = lasts[zz].astype(jnp.bfloat16)


def gather(info, batches):
    vmem = pl.BlockSpec(memory_space=pltpu.VMEM)
    flat = [ref for batch in batches for ref in batch]
    return pl.pallas_call(
        gather_kernel,
        out_shape=jax.ShapeDtypeStruct((4, 144, FINE * CH), jnp.bfloat16),
        in_specs=[pl.BlockSpec(memory_space=pltpu.SMEM)] + [vmem] * 8,
        out_specs=vmem,
        scratch_shapes=[pltpu.VMEM((4, 16, FINE * CH), jnp.float32)],
        compiler_params=pltpu.CompilerParams(vmem_limit_bytes=VMEM),
    )(info, *flat)


def finish_kernel(info_ref, own_ref, one_ref, two_ref, three_ref, out_ref, *, factor):
    total = own_ref[0, :132, :].astype(jnp.float32)
    for other in (one_ref, two_ref, three_ref):
        total += other[:132, :].astype(jnp.float32)
    total *= factor
    width = 4 * LAGS
    rows = lax.broadcasted_iota(jnp.int32, (132, width), 0)
    columns = lax.broadcasted_iota(jnp.int32, (132, width), 1)
    lag = jnp.where(rows < 128, (rows % 32) // 4 * FINE + rows // 32, LAGS - 1)
    ahead = (columns == rows % 4 * LAGS + lag).astype(jnp.float32)
    behind = (columns == rows % 4 * LAGS + LAGS - 1 - lag).astype(jnp.float32)
    for slot in range(MATCH):
        pick = jnp.where(info_ref[5 + slot] > 0, ahead, behind).astype(jnp.bfloat16)
        pieces = [total[slot * 32 : slot * 32 + 32, k * CH : (k + 1) * CH] for k in range(FINE)]
        pieces += [total[128 + slot : 129 + slot, k * CH : (k + 1) * CH] for k in range(FINE)]
        stacked = jnp.concatenate(pieces, axis=0).T
        top = stacked.astype(jnp.bfloat16)
        rest = (stacked - top.astype(jnp.float32)).astype(jnp.bfloat16)
        result = jnp.dot(top, pick, preferred_element_type=jnp.float32)
        result += jnp.dot(rest, pick, preferred_element_type=jnp.float32)
        out_ref[info_ref[1 + slot]] = result


def finish(info, own, others, factor):
    vmem = pl.BlockSpec(memory_space=pltpu.VMEM)
    return pl.pallas_call(
        functools.partial(finish_kernel, factor=factor),
        out_shape=jax.ShapeDtypeStruct((MATCH, CH, 4 * LAGS), jnp.float32),
        in_specs=[
            pl.BlockSpec(memory_space=pltpu.SMEM),
            vmem,
            vmem,
            vmem,
            vmem,
        ],
        out_specs=vmem,
    )(info, own, *others)


def exchange(series, mask):
    return lax.ppermute(series, "chan", [(block, block ^ mask) for block in range(16)])


def pass_on(block, mask):
    return lax.ppermute(block, "win", [(window, window ^ mask) for window in range(16)])


def shards(signals, plan, lag_half):
    table = jnp.asarray(quarter_table())
    own = jnp.stack([lax.axis_index("chan"), lax.axis_index("win")]).astype(jnp.int32)
    info = scalars(plan, lag_half, own)
    series, fine = whiten(signals[0], table)
    near = exchange(series, 1)
    far = exchange(series, 15)
    branches = [lambda s, a=a: exchange(s, a) for a in range(2, 15)]
    low = lax.switch(info[0] - 2, branches, series)
    high = lax.switch(info[9] - 2, branches, series)
    batches = []
    for batch, (first, second) in enumerate(((near, far), (low, high))):
        terms = correlate(info, fine, first, second, batch)
        batches.append([terms] + [pass_on(terms[d], (d >> 1) * 8 + (d & 1)) for d in (1, 2, 3)])
    sums = gather(info, batches)
    others = [pass_on(sums[d], 2 * d) for d in (1, 2, 3)]
    return finish(info, sums, others, 1.0 / math.sqrt(lax.axis_size("win") * NT))


def solution(mesh):
    placed = (P("win", "chan", None), P(), P())
    return jax.shard_map(
        shards, mesh=mesh, in_specs=placed, out_specs=P(None, "chan", "win"), check_vma=False
    )
```

```python
import functools
import math

import jax
import jax.numpy as jnp
import numpy as np
from jax import lax
from jax.experimental import pallas as pl
from jax.experimental.pallas import tpu as pltpu
from jax.sharding import PartitionSpec as P

BAND = 128
LAGS = 33
MATCH = 4
NT = 2048
BINS = NT // 2
QUART = NT // 4
HALF = BINS // 2
CH = 64
FINE = 4
COARSE = 8
MIB = 1024 * 1024


def quarter_table():
    times = np.arange(QUART, dtype=np.int64)
    freqs = np.arange(BINS, dtype=np.int64)
    angle = (times[:, None] * freqs[None, :] % NT) * (2.0 * math.pi / NT)
    return np.concatenate([np.cos(angle), np.sin(angle)], axis=1).astype(np.float32).astype(jnp.bfloat16)


def choose(plan_ref, half_ref, low_ref, high_ref, info_ref):
    own = lax.axis_index("chan")
    masks = [plan_ref[m] for m in range(MATCH)]
    high = jnp.int32(0)
    low = jnp.int32(99)
    for mask in masks:
        other = jnp.logical_and(mask != 1, mask != 15)
        low = jnp.where(other, jnp.minimum(low, mask), low)
        high = jnp.where(other, jnp.maximum(high, mask), high)
    low_ref[0] = low - 2
    high_ref[0] = high - 2
    for slot, wanted in enumerate((jnp.int32(1), low, jnp.int32(15), high)):
        place = jnp.int32(0)
        for m in range(MATCH):
            place = jnp.where(masks[m] == wanted, m, place)
        info_ref[slot : slot + 1, :] = jnp.full((1, 128), place, jnp.int32)
        info_ref[4 + slot : 5 + slot, :] = jnp.full((1, 128), 1 - 2 * half_ref[place, own], jnp.int32)


def neighbours():
    window = lax.axis_index("win")
    return (window >> 3) * 2 + (window & 1), (window >> 1) & 3


def rolled(value, shift):
    shift %= value.shape[1]
    if shift == 0:
        return value
    cut = value.shape[1] - shift
    return jnp.concatenate([value[:, cut:], value[:, :cut]], axis=1)


def whiten_kernel(
    plan_hbm, half_hbm, x_hbm, table_hbm, series_ref, low_ref, high_ref, info_ref,
    plan_ref, half_ref, x_ref, table_ref, sems,
):
    loads = [pltpu.make_async_copy(x_hbm, x_ref, sems.at[0])]
    for part in range(4):
        columns = pl.ds(part % 2 * BINS + part // 2 * HALF, HALF)
        loads.append(
            pltpu.make_async_copy(table_hbm.at[:, columns], table_ref.at[:, columns], sems.at[1 + part])
        )
    loads.append(pltpu.make_async_copy(plan_hbm, plan_ref, sems.at[5]))
    loads.append(pltpu.make_async_copy(half_hbm, half_ref, sems.at[6]))
    for load in loads:
        load.start()
    residue = lax.broadcasted_iota(jnp.int32, (CH, BAND), 1) % 4
    even = residue % 2 == 0
    alternate = jnp.where(even, 1.0, -1.0)
    halfturn = jnp.where(residue < 2, 1.0, -1.0)
    loads[0].wait()
    stacked = jnp.concatenate([x_ref[0, :, r * QUART : (r + 1) * QUART] for r in range(4)], axis=0)
    reals, sines = [], []
    for half in range(2):
        loads[1 + half * 2].wait()
        low = half * HALF
        coses = jnp.dot(stacked, table_ref[:, low : low + HALF], preferred_element_type=jnp.float32)
        loads[2 + half * 2].wait()
        low += BINS
        sinuses = jnp.dot(stacked, table_ref[:, low : low + HALF], preferred_element_type=jnp.float32)
        for band in range(HALF // BAND):
            columns = slice(band * BAND, (band + 1) * BAND)
            cos = [coses[r * CH : (r + 1) * CH, columns] for r in range(4)]
            sin = [sinuses[r * CH : (r + 1) * CH, columns] for r in range(4)]
            real = cos[0] + alternate * cos[2] + halfturn * jnp.where(even, cos[1] + cos[3], sin[3] - sin[1])
            sine = sin[0] + alternate * sin[2] + halfturn * jnp.where(even, sin[1] + sin[3], cos[1] - cos[3])
            energy = jnp.mean(real * real + sine * sine, axis=1, keepdims=True)
            factor = lax.rsqrt(energy + 1e-06)
            reals.append((real * factor).astype(jnp.bfloat16).astype(jnp.float32))
            sines.append((sine * factor).astype(jnp.bfloat16).astype(jnp.float32))
    loads[5].wait()
    loads[6].wait()
    choose(plan_ref, half_ref, low_ref, high_ref, info_ref)
    rows = []
    for r in range(4):
        cos_part, sin_part = [], []
        for real, sine in zip(reals, sines):
            if r == 0:
                u, v = real, sine
            elif r == 2:
                u, v = alternate * real, alternate * sine
            else:
                turn = halfturn if r == 1 else halfturn * alternate
                u = turn * jnp.where(even, real, sine)
                v = turn * jnp.where(even, sine, -real)
            cos_part.append(u.astype(jnp.bfloat16))
            sin_part.append(v.astype(jnp.bfloat16))
        rows.append(jnp.concatenate(cos_part + sin_part, axis=1))
    turned = jnp.concatenate(rows, axis=0)
    out = lax.dot_general(
        turned, table_ref[...], (((1,), (1,)), ((), ())), preferred_element_type=jnp.float32
    ) * BINS ** (-0.5)
    series = jnp.concatenate(
        [out[r * CH : (r + 1) * CH] for r in range(4)], axis=1
    ).astype(jnp.bfloat16)
    series_ref[...] = series


def whiten(signals, table, plan, lag_half):
    smem = pl.BlockSpec(memory_space=pltpu.SMEM)
    vmem = pl.BlockSpec(memory_space=pltpu.VMEM)
    anywhere = pl.BlockSpec(memory_space=pltpu.HBM)
    return pl.pallas_call(
        whiten_kernel,
        out_shape=[
            jax.ShapeDtypeStruct((CH, NT), jnp.bfloat16),
            jax.ShapeDtypeStruct((1,), jnp.int32),
            jax.ShapeDtypeStruct((1,), jnp.int32),
            jax.ShapeDtypeStruct((8, 128), jnp.int32),
        ],
        in_specs=[anywhere] * 4,
        out_specs=[vmem, smem, smem, vmem],
        scratch_shapes=[
            pltpu.SMEM((MATCH,), jnp.int32),
            pltpu.SMEM((MATCH, 16), jnp.int32),
            pltpu.VMEM((1, CH, NT), jnp.bfloat16),
            pltpu.VMEM((QUART, NT), jnp.bfloat16),
            pltpu.SemaphoreType.DMA((7,)),
        ],
        compiler_params=pltpu.CompilerParams(vmem_limit_bytes=60 * MIB),
    )(plan, lag_half, signals, table)


def correlate_kernel(info_ref, series_ref, first_ref, second_ref, *refs, batch):
    *out_refs, fine_ref, coarse, sums, lasts = refs
    place, _ = neighbours()
    series = series_ref[...]
    for step in range(FINE):
        fine_ref[step * CH : (step + 1) * CH, :] = rolled(series, step)
    for pair, partner_ref in enumerate((first_ref, second_ref)):
        partner = partner_ref[...]
        ahead = info_ref[4 + 2 * batch + pair : 5 + 2 * batch + pair, :1] > 0
        partner = jnp.where(ahead, partner, rolled(partner, LAGS - 1))
        for step in range(COARSE + 1):
            row = (pair * (COARSE + 1) + step) * CH
            coarse[row : row + CH, :] = rolled(partner, -FINE * step)
    main = lax.dot_general(
        coarse[...], fine_ref[...], (((1,), (1,)), ((), ())), preferred_element_type=jnp.float32
    )
    for pair in range(2):
        for q in range(16):
            group = (q >> 3) * 2 + (q & 1)
            zz = (q >> 1) & 3
            for step in range(COARSE):
                row = (pair * (COARSE + 1) + step) * CH + q * 4
                sums[group, zz * 64 + pair * 32 + step * 4 : zz * 64 + pair * 32 + step * 4 + 4, :] = main[row : row + 4, :]
            for one in range(4):
                row = (pair * (COARSE + 1) + COARSE) * CH + q * 4 + one
                lasts[group, zz * 2 + pair : zz * 2 + pair + 1, one * CH : (one + 1) * CH] = main[row : row + 1, :CH]
    for r, out_ref in enumerate(out_refs):
        out_ref[0:256, :] = sums[r ^ place].astype(jnp.bfloat16)
        out_ref[256:272, :] = lasts[r ^ place].astype(jnp.bfloat16)


def correlate(info, series, first, second, batch):
    vmem = pl.BlockSpec(memory_space=pltpu.VMEM)
    return pl.pallas_call(
        functools.partial(correlate_kernel, batch=batch),
        out_shape=[jax.ShapeDtypeStruct((272, FINE * CH), jnp.bfloat16)] * 4,
        in_specs=[vmem] * 4,
        out_specs=[vmem] * 4,
        scratch_shapes=[
            pltpu.VMEM((FINE * CH, NT), jnp.bfloat16),
            pltpu.VMEM((2 * (COARSE + 1) * CH, NT), jnp.bfloat16),
            pltpu.VMEM((4, 256, FINE * CH), jnp.float32),
            pltpu.VMEM((4, 16, FINE * CH), jnp.float32),
        ],
        compiler_params=pltpu.CompilerParams(vmem_limit_bytes=24 * MIB),
        cost_estimate=pl.CostEstimate(flops=4 * CH * CH * LAGS * NT, bytes_accessed=4 << 20, transcendentals=0),
    )(info, series, first, second)


def gather_kernel(own_ref, one_ref, two_ref, three_ref, *refs):
    *out_refs, sums = refs
    _, place = neighbours()

    def total(rows):
        result = own_ref[rows, :].astype(jnp.float32)
        for other in (one_ref, two_ref, three_ref):
            result += other[rows, :].astype(jnp.float32)
        return result

    last = total(slice(256, 272))
    for zz in range(4):
        sums[zz, 0:64, :] = total(slice(zz * 64, zz * 64 + 64))
        sums[zz, 64:66, :] = last[zz * 2 : zz * 2 + 2, :]
    for r, out_ref in enumerate(out_refs):
        out_ref[...] = sums[r ^ place].astype(jnp.bfloat16)


def gather(terms):
    vmem = pl.BlockSpec(memory_space=pltpu.VMEM)
    return pl.pallas_call(
        gather_kernel,
        out_shape=[jax.ShapeDtypeStruct((80, FINE * CH), jnp.bfloat16)] * 4,
        in_specs=[vmem] * 4,
        out_specs=[vmem] * 4,
        scratch_shapes=[pltpu.VMEM((4, 80, FINE * CH), jnp.float32)],
        compiler_params=pltpu.CompilerParams(vmem_limit_bytes=16 * MIB),
    )(*terms)


def finish_kernel(info_ref, *refs, factor):
    out_ref = refs[8]
    width = 4 * LAGS
    rows = lax.broadcasted_iota(jnp.int32, (132, width), 0)
    columns = lax.broadcasted_iota(jnp.int32, (132, width), 1)
    lag = jnp.where(rows < 128, (rows % 32) // 4 * FINE + rows // 32, LAGS - 1)
    ahead = (columns == rows % 4 * LAGS + lag).astype(jnp.float32)
    behind = (columns == rows % 4 * LAGS + LAGS - 1 - lag).astype(jnp.float32)
    for batch in range(2):
        own_ref, *others = refs[batch * 4 : batch * 4 + 4]
        total = own_ref[:66, :].astype(jnp.float32)
        for other in others:
            total += other[:66, :].astype(jnp.float32)
        total *= factor
        for pair in range(2):
            slot = batch * 2 + pair
            pick = jnp.where(info_ref[4 + slot : 5 + slot, :1] > 0, ahead, behind).astype(jnp.bfloat16)
            pieces = [total[pair * 32 : pair * 32 + 32, k * CH : (k + 1) * CH] for k in range(FINE)]
            pieces += [total[64 + pair : 65 + pair, k * CH : (k + 1) * CH] for k in range(FINE)]
            stacked = jnp.concatenate(pieces, axis=0).T
            top = stacked.astype(jnp.bfloat16)
            rest = (stacked - top.astype(jnp.float32)).astype(jnp.bfloat16)
            result = jnp.dot(top, pick, preferred_element_type=jnp.float32)
            result += jnp.dot(rest, pick, preferred_element_type=jnp.float32)
            out_ref[jnp.max(info_ref[slot : slot + 1, :])] = result


def finish(info, terms, factor):
    vmem = pl.BlockSpec(memory_space=pltpu.VMEM)
    return pl.pallas_call(
        functools.partial(finish_kernel, factor=factor),
        out_shape=jax.ShapeDtypeStruct((MATCH, CH, 4 * LAGS), jnp.float32),
        in_specs=[vmem] * 9,
        out_specs=vmem,
        compiler_params=pltpu.CompilerParams(vmem_limit_bytes=16 * MIB),
    )(info, *terms)


def exchange(series, mask):
    return lax.ppermute(series, "chan", [(block, block ^ mask) for block in range(16)])


def pass_on(block, mask):
    return lax.ppermute(block, "win", [(window, window ^ mask) for window in range(16)])


def to_neighbours(terms):
    return [terms[0]] + [pass_on(terms[d], (d >> 1) * 8 + (d & 1)) for d in (1, 2, 3)]


def along_z(sums):
    return [sums[0]] + [pass_on(sums[d], 2 * d) for d in (1, 2, 3)]


def shards(signals, plan, lag_half):
    table = jnp.asarray(quarter_table())
    series, first, second, info = whiten(signals, table, plan, lag_half)
    branches = [lambda s, a=a: exchange(s, a) for a in range(2, 15)]
    near = exchange(series, 1)
    low = lax.switch(first.reshape(()), branches, series)
    later, low = lax.optimization_barrier((series, low))
    far = exchange(later, 15)
    terms = correlate(info, series, near, low, 0)
    later, terms = lax.optimization_barrier((series, terms))
    high = lax.switch(second.reshape(()), branches, later)
    terms, high = lax.optimization_barrier((to_neighbours(terms), high))
    sums = gather(terms)
    far, high, sums = lax.optimization_barrier((far, high, sums))
    last_sums = gather(to_neighbours(correlate(info, series, far, high, 1)))
    return finish(info, along_z(sums) + along_z(last_sums), 1.0 / math.sqrt(lax.axis_size("win") * NT))


def solution(mesh):
    placed = (P("win", "chan", None), P(), P())
    return jax.shard_map(
        shards, mesh=mesh, in_specs=placed, out_specs=P(None, "chan", "win"), check_vma=False
    )
```

```python
import functools
import math

import jax
import jax.numpy as jnp
import numpy as np
from jax import lax
from jax.experimental import pallas as pl
from jax.experimental.pallas import tpu as pltpu
from jax.sharding import PartitionSpec as P

BAND = 128
LAGS = 33
MATCH = 4
NT = 2048
BINS = NT // 2
QUART = NT // 4
HALF = BINS // 2
CH = 64
FINE = 4
COARSE = 8
MIB = 1024 * 1024


def quarter_table():
    times = np.arange(QUART, dtype=np.int64)
    freqs = np.arange(BINS, dtype=np.int64)
    angle = (times[:, None] * freqs[None, :] % NT) * (2.0 * math.pi / NT)
    return np.concatenate([np.cos(angle), np.sin(angle)], axis=1).astype(np.float32).astype(jnp.bfloat16)


def choose(plan_ref, half_ref, low_ref, high_ref, info_ref):
    own = lax.axis_index("chan")
    masks = [plan_ref[m] for m in range(MATCH)]
    high = jnp.int32(0)
    low = jnp.int32(99)
    for mask in masks:
        other = jnp.logical_and(mask != 1, mask != 15)
        key = mask + 16 * (1 - ((mask >> 1) & 1))
        low = jnp.where(other, jnp.minimum(low, key), low)
        high = jnp.where(other, jnp.maximum(high, key), high)
    low = low & 15
    high = high & 15
    low_ref[0] = low - 2
    high_ref[0] = high - 2
    for slot, wanted in enumerate((jnp.int32(1), low, jnp.int32(15), high)):
        place = jnp.int32(0)
        for m in range(MATCH):
            place = jnp.where(masks[m] == wanted, m, place)
        info_ref[slot : slot + 1, :] = jnp.full((1, 128), place, jnp.int32)
        info_ref[4 + slot : 5 + slot, :] = jnp.full((1, 128), 1 - 2 * half_ref[place, own], jnp.int32)


def neighbours():
    window = lax.axis_index("win")
    return (window >> 3) * 2 + (window & 1), (window >> 1) & 3


def rolled(value, shift):
    shift %= value.shape[1]
    if shift == 0:
        return value
    cut = value.shape[1] - shift
    return jnp.concatenate([value[:, cut:], value[:, :cut]], axis=1)


def whiten_kernel(
    plan_hbm, half_hbm, x_hbm, table_hbm, series_ref, low_ref, high_ref, info_ref,
    plan_ref, half_ref, x_ref, table_ref, sems,
):
    loads = [pltpu.make_async_copy(x_hbm, x_ref, sems.at[0])]
    for part in range(4):
        columns = pl.ds(part % 2 * BINS + part // 2 * HALF, HALF)
        loads.append(
            pltpu.make_async_copy(table_hbm.at[:, columns], table_ref.at[:, columns], sems.at[1 + part])
        )
    loads.append(pltpu.make_async_copy(plan_hbm, plan_ref, sems.at[5]))
    loads.append(pltpu.make_async_copy(half_hbm, half_ref, sems.at[6]))
    for load in loads:
        load.start()
    residue = lax.broadcasted_iota(jnp.int32, (CH, BAND), 1) % 4
    even = residue % 2 == 0
    alternate = jnp.where(even, 1.0, -1.0)
    halfturn = jnp.where(residue < 2, 1.0, -1.0)
    loads[0].wait()
    stacked = jnp.concatenate([x_ref[0, :, r * QUART : (r + 1) * QUART] for r in range(4)], axis=0)
    reals, sines = [], []
    for half in range(2):
        loads[1 + half * 2].wait()
        low = half * HALF
        coses = jnp.dot(stacked, table_ref[:, low : low + HALF], preferred_element_type=jnp.float32)
        loads[2 + half * 2].wait()
        low += BINS
        sinuses = jnp.dot(stacked, table_ref[:, low : low + HALF], preferred_element_type=jnp.float32)
        for band in range(HALF // BAND):
            columns = slice(band * BAND, (band + 1) * BAND)
            cos = [coses[r * CH : (r + 1) * CH, columns] for r in range(4)]
            sin = [sinuses[r * CH : (r + 1) * CH, columns] for r in range(4)]
            real = cos[0] + alternate * cos[2] + halfturn * jnp.where(even, cos[1] + cos[3], sin[3] - sin[1])
            sine = sin[0] + alternate * sin[2] + halfturn * jnp.where(even, sin[1] + sin[3], cos[1] - cos[3])
            energy = jnp.mean(real * real + sine * sine, axis=1, keepdims=True)
            factor = lax.rsqrt(energy + 1e-06)
            reals.append((real * factor).astype(jnp.bfloat16).astype(jnp.float32))
            sines.append((sine * factor).astype(jnp.bfloat16).astype(jnp.float32))
    loads[5].wait()
    loads[6].wait()
    choose(plan_ref, half_ref, low_ref, high_ref, info_ref)
    rows = []
    for r in range(4):
        cos_part, sin_part = [], []
        for real, sine in zip(reals, sines):
            if r == 0:
                u, v = real, sine
            elif r == 2:
                u, v = alternate * real, alternate * sine
            else:
                turn = halfturn if r == 1 else halfturn * alternate
                u = turn * jnp.where(even, real, sine)
                v = turn * jnp.where(even, sine, -real)
            cos_part.append(u.astype(jnp.bfloat16))
            sin_part.append(v.astype(jnp.bfloat16))
        rows.append(jnp.concatenate(cos_part + sin_part, axis=1))
    turned = jnp.concatenate(rows, axis=0)
    out = lax.dot_general(
        turned, table_ref[...], (((1,), (1,)), ((), ())), preferred_element_type=jnp.float32
    ) * BINS ** (-0.5)
    series = jnp.concatenate(
        [out[r * CH : (r + 1) * CH] for r in range(4)], axis=1
    ).astype(jnp.bfloat16)
    series_ref[...] = series


def whiten(signals, table, plan, lag_half):
    smem = pl.BlockSpec(memory_space=pltpu.SMEM)
    vmem = pl.BlockSpec(memory_space=pltpu.VMEM)
    anywhere = pl.BlockSpec(memory_space=pltpu.HBM)
    return pl.pallas_call(
        whiten_kernel,
        out_shape=[
            jax.ShapeDtypeStruct((CH, NT), jnp.bfloat16),
            jax.ShapeDtypeStruct((1,), jnp.int32),
            jax.ShapeDtypeStruct((1,), jnp.int32),
            jax.ShapeDtypeStruct((8, 128), jnp.int32),
        ],
        in_specs=[anywhere] * 4,
        out_specs=[vmem, smem, smem, vmem],
        scratch_shapes=[
            pltpu.SMEM((MATCH,), jnp.int32),
            pltpu.SMEM((MATCH, 16), jnp.int32),
            pltpu.VMEM((1, CH, NT), jnp.bfloat16),
            pltpu.VMEM((QUART, NT), jnp.bfloat16),
            pltpu.SemaphoreType.DMA((7,)),
        ],
        compiler_params=pltpu.CompilerParams(vmem_limit_bytes=60 * MIB),
    )(plan, lag_half, signals, table)


def correlate_kernel(info_ref, series_ref, first_ref, second_ref, *refs, batch):
    *out_refs, fine_ref, coarse, sums, lasts = refs
    place, _ = neighbours()
    series = series_ref[...]
    for step in range(FINE):
        fine_ref[step * CH : (step + 1) * CH, :] = rolled(series, step)
    for pair, partner_ref in enumerate((first_ref, second_ref)):
        partner = partner_ref[...]
        ahead = info_ref[4 + 2 * batch + pair : 5 + 2 * batch + pair, :1] > 0
        partner = jnp.where(ahead, partner, rolled(partner, LAGS - 1))
        for step in range(COARSE + 1):
            row = (pair * (COARSE + 1) + step) * CH
            coarse[row : row + CH, :] = rolled(partner, -FINE * step)
    main = lax.dot_general(
        coarse[...], fine_ref[...], (((1,), (1,)), ((), ())), preferred_element_type=jnp.float32
    )
    for pair in range(2):
        for q in range(16):
            group = (q >> 3) * 2 + (q & 1)
            zz = (q >> 1) & 3
            for step in range(COARSE):
                row = (pair * (COARSE + 1) + step) * CH + q * 4
                sums[group, zz * 64 + pair * 32 + step * 4 : zz * 64 + pair * 32 + step * 4 + 4, :] = main[row : row + 4, :]
            for one in range(4):
                row = (pair * (COARSE + 1) + COARSE) * CH + q * 4 + one
                lasts[group, zz * 2 + pair : zz * 2 + pair + 1, one * CH : (one + 1) * CH] = main[row : row + 1, :CH]
    for r, out_ref in enumerate(out_refs):
        out_ref[0:256, :] = sums[r ^ place].astype(jnp.bfloat16)
        out_ref[256:272, :] = lasts[r ^ place].astype(jnp.bfloat16)


def correlate(info, series, first, second, batch):
    vmem = pl.BlockSpec(memory_space=pltpu.VMEM)
    return pl.pallas_call(
        functools.partial(correlate_kernel, batch=batch),
        out_shape=[jax.ShapeDtypeStruct((272, FINE * CH), jnp.bfloat16)] * 4,
        in_specs=[vmem] * 4,
        out_specs=[vmem] * 4,
        scratch_shapes=[
            pltpu.VMEM((FINE * CH, NT), jnp.bfloat16),
            pltpu.VMEM((2 * (COARSE + 1) * CH, NT), jnp.bfloat16),
            pltpu.VMEM((4, 256, FINE * CH), jnp.float32),
            pltpu.VMEM((4, 16, FINE * CH), jnp.float32),
        ],
        compiler_params=pltpu.CompilerParams(vmem_limit_bytes=24 * MIB),
        cost_estimate=pl.CostEstimate(flops=4 * CH * CH * LAGS * NT, bytes_accessed=4 << 20, transcendentals=0),
    )(info, series, first, second)


def gather_kernel(own_ref, one_ref, two_ref, three_ref, *refs):
    *out_refs, sums = refs
    _, place = neighbours()

    def total(rows):
        result = own_ref[rows, :].astype(jnp.float32)
        for other in (one_ref, two_ref, three_ref):
            result += other[rows, :].astype(jnp.float32)
        return result

    last = total(slice(256, 272))
    for zz in range(4):
        sums[zz, 0:64, :] = total(slice(zz * 64, zz * 64 + 64))
        sums[zz, 64:66, :] = last[zz * 2 : zz * 2 + 2, :]
    for r, out_ref in enumerate(out_refs):
        out_ref[...] = sums[r ^ place].astype(jnp.bfloat16)


def gather(terms):
    vmem = pl.BlockSpec(memory_space=pltpu.VMEM)
    return pl.pallas_call(
        gather_kernel,
        out_shape=[jax.ShapeDtypeStruct((80, FINE * CH), jnp.bfloat16)] * 4,
        in_specs=[vmem] * 4,
        out_specs=[vmem] * 4,
        scratch_shapes=[pltpu.VMEM((4, 80, FINE * CH), jnp.float32)],
        compiler_params=pltpu.CompilerParams(vmem_limit_bytes=16 * MIB),
    )(*terms)


def finish_kernel(info_ref, *refs, factor):
    out_ref = refs[8]
    width = 4 * LAGS
    rows = lax.broadcasted_iota(jnp.int32, (132, width), 0)
    columns = lax.broadcasted_iota(jnp.int32, (132, width), 1)
    lag = jnp.where(rows < 128, (rows % 32) // 4 * FINE + rows // 32, LAGS - 1)
    ahead = (columns == rows % 4 * LAGS + lag).astype(jnp.float32)
    behind = (columns == rows % 4 * LAGS + LAGS - 1 - lag).astype(jnp.float32)
    for batch in range(2):
        own_ref, *others = refs[batch * 4 : batch * 4 + 4]
        total = own_ref[:66, :].astype(jnp.float32)
        for other in others:
            total += other[:66, :].astype(jnp.float32)
        total *= factor
        for pair in range(2):
            slot = batch * 2 + pair
            pick = jnp.where(info_ref[4 + slot : 5 + slot, :1] > 0, ahead, behind).astype(jnp.bfloat16)
            pieces = [total[pair * 32 : pair * 32 + 32, k * CH : (k + 1) * CH] for k in range(FINE)]
            pieces += [total[64 + pair : 65 + pair, k * CH : (k + 1) * CH] for k in range(FINE)]
            stacked = jnp.concatenate(pieces, axis=0).T
            top = stacked.astype(jnp.bfloat16)
            rest = (stacked - top.astype(jnp.float32)).astype(jnp.bfloat16)
            result = jnp.dot(top, pick, preferred_element_type=jnp.float32)
            result += jnp.dot(rest, pick, preferred_element_type=jnp.float32)
            out_ref[jnp.max(info_ref[slot : slot + 1, :])] = result


def finish(info, terms, factor):
    vmem = pl.BlockSpec(memory_space=pltpu.VMEM)
    return pl.pallas_call(
        functools.partial(finish_kernel, factor=factor),
        out_shape=jax.ShapeDtypeStruct((MATCH, CH, 4 * LAGS), jnp.float32),
        in_specs=[vmem] * 9,
        out_specs=vmem,
        compiler_params=pltpu.CompilerParams(vmem_limit_bytes=16 * MIB),
    )(info, *terms)


def exchange(series, mask):
    return lax.ppermute(series, "chan", [(block, block ^ mask) for block in range(16)])


def pass_on(block, mask):
    return lax.ppermute(block, "win", [(window, window ^ mask) for window in range(16)])


def to_neighbours(terms):
    return [terms[0]] + [pass_on(terms[d], (d >> 1) * 8 + (d & 1)) for d in (1, 2, 3)]


def along_z(sums):
    return [sums[0]] + [pass_on(sums[d], 2 * d) for d in (1, 2, 3)]


def shards(signals, plan, lag_half):
    table = jnp.asarray(quarter_table())
    series, first, second, info = whiten(signals, table, plan, lag_half)
    branches = [lambda s, a=a: exchange(s, a) for a in range(2, 15)]
    near = exchange(series, 1)
    low = lax.switch(first.reshape(()), branches, series)
    later, low = lax.optimization_barrier((series, low))
    far = exchange(later, 15)
    terms = correlate(info, series, near, low, 0)
    later, terms = lax.optimization_barrier((series, terms))
    high = lax.switch(second.reshape(()), branches, later)
    terms, high = lax.optimization_barrier((to_neighbours(terms), high))
    sums = gather(terms)
    far, high, sums = lax.optimization_barrier((far, high, sums))
    last_sums = gather(to_neighbours(correlate(info, series, far, high, 1)))
    return finish(info, along_z(sums) + along_z(last_sums), 1.0 / math.sqrt(lax.axis_size("win") * NT))


def solution(mesh):
    placed = (P("win", "chan", None), P(), P())
    return jax.shard_map(
        shards, mesh=mesh, in_specs=placed, out_specs=P(None, "chan", "win"), check_vma=False
    )
```

```python
import functools
import math

import jax
import jax.numpy as jnp
import numpy as np
from jax import lax
from jax.experimental import pallas as pl
from jax.experimental.pallas import tpu as pltpu
from jax.sharding import PartitionSpec as P

BAND = 128
LAGS = 33
MATCH = 4
NT = 2048
BINS = NT // 2
QUART = NT // 4
HALF = BINS // 2
CH = 64
FINE = 4
COARSE = 8
MIB = 1024 * 1024


def quarter_table():
    times = np.arange(QUART, dtype=np.int64)
    freqs = np.arange(BINS, dtype=np.int64)
    angle = (times[:, None] * freqs[None, :] % NT) * (2.0 * math.pi / NT)
    return np.concatenate([np.cos(angle), np.sin(angle)], axis=1).astype(np.float32).astype(jnp.bfloat16)


def choose(plan_ref, half_ref, low_ref, high_ref, info_ref):
    own = lax.axis_index("chan")
    masks = [plan_ref[m] for m in range(MATCH)]
    high = jnp.int32(0)
    low = jnp.int32(99)
    for mask in masks:
        other = jnp.logical_and(mask != 1, mask != 15)
        key = mask + 16 * (1 - ((mask >> 1) & 1))
        low = jnp.where(other, jnp.minimum(low, key), low)
        high = jnp.where(other, jnp.maximum(high, key), high)
    low = low & 15
    high = high & 15
    low_ref[0] = low - 2
    high_ref[0] = high - 2
    for slot, wanted in enumerate((jnp.int32(1), low, jnp.int32(15), high)):
        place = jnp.int32(0)
        for m in range(MATCH):
            place = jnp.where(masks[m] == wanted, m, place)
        info_ref[slot : slot + 1, :] = jnp.full((1, 128), place, jnp.int32)
        info_ref[4 + slot : 5 + slot, :] = jnp.full((1, 128), 1 - 2 * half_ref[place, own], jnp.int32)


def neighbours():
    window = lax.axis_index("win")
    return (window >> 3) * 2 + (window & 1), (window >> 1) & 3


def rolled(value, shift):
    shift %= value.shape[1]
    if shift == 0:
        return value
    cut = value.shape[1] - shift
    return jnp.concatenate([value[:, cut:], value[:, :cut]], axis=1)


def whiten_kernel(
    plan_hbm, half_hbm, x_hbm, table_hbm, series_ref, low_ref, high_ref, info_ref,
    plan_ref, half_ref, x_ref, table_ref, sems,
):
    loads = [pltpu.make_async_copy(x_hbm, x_ref, sems.at[0])]
    for part in range(4):
        columns = pl.ds(part % 2 * BINS + part // 2 * HALF, HALF)
        loads.append(
            pltpu.make_async_copy(table_hbm.at[:, columns], table_ref.at[:, columns], sems.at[1 + part])
        )
    loads.append(pltpu.make_async_copy(plan_hbm, plan_ref, sems.at[5]))
    loads.append(pltpu.make_async_copy(half_hbm, half_ref, sems.at[6]))
    for load in loads:
        load.start()
    residue = lax.broadcasted_iota(jnp.int32, (CH, BAND), 1) % 4
    even = residue % 2 == 0
    alternate = jnp.where(even, 1.0, -1.0)
    halfturn = jnp.where(residue < 2, 1.0, -1.0)
    loads[0].wait()
    stacked = jnp.concatenate([x_ref[0, :, r * QUART : (r + 1) * QUART] for r in range(4)], axis=0)
    reals, sines = [], []
    for half in range(2):
        loads[1 + half * 2].wait()
        low = half * HALF
        coses = jnp.dot(stacked, table_ref[:, low : low + HALF], preferred_element_type=jnp.float32)
        loads[2 + half * 2].wait()
        low += BINS
        sinuses = jnp.dot(stacked, table_ref[:, low : low + HALF], preferred_element_type=jnp.float32)
        for band in range(HALF // BAND):
            columns = slice(band * BAND, (band + 1) * BAND)
            cos = [coses[r * CH : (r + 1) * CH, columns] for r in range(4)]
            sin = [sinuses[r * CH : (r + 1) * CH, columns] for r in range(4)]
            real = cos[0] + alternate * cos[2] + halfturn * jnp.where(even, cos[1] + cos[3], sin[3] - sin[1])
            sine = sin[0] + alternate * sin[2] + halfturn * jnp.where(even, sin[1] + sin[3], cos[1] - cos[3])
            energy = jnp.mean(real * real + sine * sine, axis=1, keepdims=True)
            factor = lax.rsqrt(energy + 1e-06)
            reals.append((real * factor).astype(jnp.bfloat16).astype(jnp.float32))
            sines.append((sine * factor).astype(jnp.bfloat16).astype(jnp.float32))
    loads[5].wait()
    loads[6].wait()
    choose(plan_ref, half_ref, low_ref, high_ref, info_ref)
    rows = []
    for r in range(4):
        cos_part, sin_part = [], []
        for real, sine in zip(reals, sines):
            if r == 0:
                u, v = real, sine
            elif r == 2:
                u, v = alternate * real, alternate * sine
            else:
                turn = halfturn if r == 1 else halfturn * alternate
                u = turn * jnp.where(even, real, sine)
                v = turn * jnp.where(even, sine, -real)
            cos_part.append(u.astype(jnp.bfloat16))
            sin_part.append(v.astype(jnp.bfloat16))
        rows.append(jnp.concatenate(cos_part + sin_part, axis=1))
    turned = jnp.concatenate(rows, axis=0)
    out = lax.dot_general(
        turned, table_ref[...], (((1,), (1,)), ((), ())), preferred_element_type=jnp.float32
    ) * BINS ** (-0.5)
    series = jnp.concatenate(
        [out[r * CH : (r + 1) * CH] for r in range(4)], axis=1
    ).astype(jnp.bfloat16)
    series_ref[...] = series


def whiten(signals, table, plan, lag_half):
    smem = pl.BlockSpec(memory_space=pltpu.SMEM)
    vmem = pl.BlockSpec(memory_space=pltpu.VMEM)
    anywhere = pl.BlockSpec(memory_space=pltpu.HBM)
    return pl.pallas_call(
        whiten_kernel,
        out_shape=[
            jax.ShapeDtypeStruct((CH, NT), jnp.bfloat16),
            jax.ShapeDtypeStruct((1,), jnp.int32),
            jax.ShapeDtypeStruct((1,), jnp.int32),
            jax.ShapeDtypeStruct((8, 128), jnp.int32),
        ],
        in_specs=[anywhere] * 4,
        out_specs=[vmem, smem, smem, vmem],
        scratch_shapes=[
            pltpu.SMEM((MATCH,), jnp.int32),
            pltpu.SMEM((MATCH, 16), jnp.int32),
            pltpu.VMEM((1, CH, NT), jnp.bfloat16),
            pltpu.VMEM((QUART, NT), jnp.bfloat16),
            pltpu.SemaphoreType.DMA((7,)),
        ],
        compiler_params=pltpu.CompilerParams(vmem_limit_bytes=60 * MIB),
    )(plan, lag_half, signals, table)


def correlate_kernel(info_ref, series_ref, first_ref, second_ref, *refs, batch):
    *out_refs, fine_ref, coarse, sums, lasts = refs
    place, _ = neighbours()
    series = series_ref[...]
    for step in range(FINE):
        fine_ref[step * CH : (step + 1) * CH, :] = rolled(series, step)
    for pair, partner_ref in enumerate((first_ref, second_ref)):
        partner = partner_ref[...]
        ahead = info_ref[4 + 2 * batch + pair : 5 + 2 * batch + pair, :1] > 0
        partner = jnp.where(ahead, partner, rolled(partner, LAGS - 1))
        for step in range(COARSE + 1):
            row = (pair * (COARSE + 1) + step) * CH
            coarse[row : row + CH, :] = rolled(partner, -FINE * step)
    main = lax.dot_general(
        coarse[...], fine_ref[...], (((1,), (1,)), ((), ())), preferred_element_type=jnp.float32
    )
    for pair in range(2):
        for q in range(16):
            group = (q >> 3) * 2 + (q & 1)
            zz = (q >> 1) & 3
            for step in range(COARSE):
                row = (pair * (COARSE + 1) + step) * CH + q * 4
                sums[group, zz * 64 + pair * 32 + step * 4 : zz * 64 + pair * 32 + step * 4 + 4, :] = main[row : row + 4, :]
            for one in range(4):
                row = (pair * (COARSE + 1) + COARSE) * CH + q * 4 + one
                lasts[group, zz * 2 + pair : zz * 2 + pair + 1, one * CH : (one + 1) * CH] = main[row : row + 1, :CH]
    for r, out_ref in enumerate(out_refs):
        out_ref[0:256, :] = sums[r ^ place].astype(jnp.bfloat16)
        out_ref[256:272, :] = lasts[r ^ place].astype(jnp.bfloat16)


def correlate(info, series, first, second, batch):
    vmem = pl.BlockSpec(memory_space=pltpu.VMEM)
    return pl.pallas_call(
        functools.partial(correlate_kernel, batch=batch),
        out_shape=[jax.ShapeDtypeStruct((272, FINE * CH), jnp.bfloat16)] * 4,
        in_specs=[vmem] * 4,
        out_specs=[vmem] * 4,
        scratch_shapes=[
            pltpu.VMEM((FINE * CH, NT), jnp.bfloat16),
            pltpu.VMEM((2 * (COARSE + 1) * CH, NT), jnp.bfloat16),
            pltpu.VMEM((4, 256, FINE * CH), jnp.float32),
            pltpu.VMEM((4, 16, FINE * CH), jnp.float32),
        ],
        compiler_params=pltpu.CompilerParams(vmem_limit_bytes=24 * MIB),
        cost_estimate=pl.CostEstimate(flops=4 * CH * CH * LAGS * NT, bytes_accessed=4 << 20, transcendentals=0),
    )(info, series, first, second)


def gather_kernel(own_ref, one_ref, two_ref, three_ref, *refs):
    *out_refs, sums = refs
    _, place = neighbours()

    def total(rows):
        result = own_ref[rows, :].astype(jnp.float32)
        for other in (one_ref, two_ref, three_ref):
            result += other[rows, :].astype(jnp.float32)
        return result

    last = total(slice(256, 272))
    for zz in range(4):
        sums[zz, 0:64, :] = total(slice(zz * 64, zz * 64 + 64))
        sums[zz, 64:66, :] = last[zz * 2 : zz * 2 + 2, :]
    for r, out_ref in enumerate(out_refs):
        out_ref[...] = sums[r ^ place].astype(jnp.bfloat16)


def gather(terms):
    vmem = pl.BlockSpec(memory_space=pltpu.VMEM)
    return pl.pallas_call(
        gather_kernel,
        out_shape=[jax.ShapeDtypeStruct((80, FINE * CH), jnp.bfloat16)] * 4,
        in_specs=[vmem] * 4,
        out_specs=[vmem] * 4,
        scratch_shapes=[pltpu.VMEM((4, 80, FINE * CH), jnp.float32)],
        compiler_params=pltpu.CompilerParams(vmem_limit_bytes=16 * MIB),
    )(*terms)


def finish_kernel(info_ref, *refs, factor):
    out_ref = refs[8]
    width = 4 * LAGS
    rows = lax.broadcasted_iota(jnp.int32, (132, width), 0)
    columns = lax.broadcasted_iota(jnp.int32, (132, width), 1)
    lag = jnp.where(rows < 128, (rows % 32) // 4 * FINE + rows // 32, LAGS - 1)
    ahead = (columns == rows % 4 * LAGS + lag).astype(jnp.float32)
    behind = (columns == rows % 4 * LAGS + LAGS - 1 - lag).astype(jnp.float32)
    for batch in range(2):
        own_ref, *others = refs[batch * 4 : batch * 4 + 4]
        total = own_ref[:66, :].astype(jnp.float32)
        for other in others:
            total += other[:66, :].astype(jnp.float32)
        total *= factor
        for pair in range(2):
            slot = batch * 2 + pair
            pick = jnp.where(info_ref[4 + slot : 5 + slot, :1] > 0, ahead, behind).astype(jnp.bfloat16)
            pieces = [total[pair * 32 : pair * 32 + 32, k * CH : (k + 1) * CH] for k in range(FINE)]
            pieces += [total[64 + pair : 65 + pair, k * CH : (k + 1) * CH] for k in range(FINE)]
            stacked = jnp.concatenate(pieces, axis=0).T
            top = stacked.astype(jnp.bfloat16)
            rest = (stacked - top.astype(jnp.float32)).astype(jnp.bfloat16)
            result = jnp.dot(top, pick, preferred_element_type=jnp.float32)
            result += jnp.dot(rest, pick, preferred_element_type=jnp.float32)
            out_ref[jnp.max(info_ref[slot : slot + 1, :])] = result


def finish(info, terms, factor):
    vmem = pl.BlockSpec(memory_space=pltpu.VMEM)
    return pl.pallas_call(
        functools.partial(finish_kernel, factor=factor),
        out_shape=jax.ShapeDtypeStruct((MATCH, CH, 4 * LAGS), jnp.float32),
        in_specs=[vmem] * 9,
        out_specs=vmem,
        compiler_params=pltpu.CompilerParams(vmem_limit_bytes=16 * MIB),
    )(info, *terms)


def exchange(series, mask):
    return lax.ppermute(series, "chan", [(block, block ^ mask) for block in range(16)])


def pass_on(block, mask):
    return lax.ppermute(block, "win", [(window, window ^ mask) for window in range(16)])


def to_neighbours(terms):
    return [terms[0]] + [pass_on(terms[d], (d >> 1) * 8 + (d & 1)) for d in (1, 2, 3)]


def along_z(sums):
    return [sums[0]] + [pass_on(sums[d], 2 * d) for d in (2, 1, 3)]


def shards(signals, plan, lag_half):
    table = jnp.asarray(quarter_table())
    series, first, second, info = whiten(signals, table, plan, lag_half)
    branches = [lambda s, a=a: exchange(s, a) for a in range(2, 15)]
    near = exchange(series, 1)
    low = lax.switch(first.reshape(()), branches, series)
    later, low = lax.optimization_barrier((series, low))
    far = exchange(later, 15)
    terms = correlate(info, series, near, low, 0)
    later, terms = lax.optimization_barrier((series, terms))
    high = lax.switch(second.reshape(()), branches, later)
    terms, high = lax.optimization_barrier((to_neighbours(terms), high))
    sums = gather(terms)
    far, high, sums = lax.optimization_barrier((far, high, sums))
    last_sums = gather(to_neighbours(correlate(info, series, far, high, 1)))
    return finish(info, along_z(sums) + along_z(last_sums), 1.0 / math.sqrt(lax.axis_size("win") * NT))


def solution(mesh):
    placed = (P("win", "chan", None), P(), P())
    return jax.shard_map(
        shards, mesh=mesh, in_specs=placed, out_specs=P(None, "chan", "win"), check_vma=False
    )
```

```python
import functools
import math

import jax
import jax.numpy as jnp
import numpy as np
from jax import lax
from jax.experimental import pallas as pl
from jax.experimental.pallas import tpu as pltpu
from jax.sharding import PartitionSpec as P

BAND = 128
LAGS = 33
MATCH = 4
NT = 2048
BINS = NT // 2
QUART = NT // 4
HALF = BINS // 2
CH = 64
FINE = 4
COARSE = 8
MIB = 1024 * 1024


def quarter_table():
    times = np.arange(QUART, dtype=np.int64)
    freqs = np.arange(BINS, dtype=np.int64)
    angle = (times[:, None] * freqs[None, :] % NT) * (2.0 * math.pi / NT)
    return np.concatenate([np.cos(angle), np.sin(angle)], axis=1).astype(np.float32).astype(jnp.bfloat16)


def choose(plan_ref, half_ref, low_ref, high_ref, info_ref):
    own = lax.axis_index("chan")
    masks = [plan_ref[m] for m in range(MATCH)]
    high = jnp.int32(0)
    low = jnp.int32(99)
    for mask in masks:
        other = jnp.logical_and(mask != 1, mask != 15)
        key = mask + 16 * (1 - ((mask >> 1) & 1))
        low = jnp.where(other, jnp.minimum(low, key), low)
        high = jnp.where(other, jnp.maximum(high, key), high)
    low = low & 15
    high = high & 15
    low_ref[0] = low - 2
    high_ref[0] = high - 2
    for slot, wanted in enumerate((jnp.int32(1), low, jnp.int32(15), high)):
        place = jnp.int32(0)
        for m in range(MATCH):
            place = jnp.where(masks[m] == wanted, m, place)
        info_ref[slot : slot + 1, :] = jnp.full((1, 128), place, jnp.int32)
        info_ref[4 + slot : 5 + slot, :] = jnp.full((1, 128), 1 - 2 * half_ref[place, own], jnp.int32)


def neighbours():
    window = lax.axis_index("win")
    return (window >> 3) * 2 + (window & 1), (window >> 1) & 3


def rolled(value, shift):
    shift %= value.shape[1]
    if shift == 0:
        return value
    cut = value.shape[1] - shift
    return jnp.concatenate([value[:, cut:], value[:, :cut]], axis=1)


def whiten_kernel(
    plan_hbm, half_hbm, x_hbm, table_hbm, series_ref, low_ref, high_ref, info_ref,
    plan_ref, half_ref, x_ref, table_ref, sems,
):
    loads = [pltpu.make_async_copy(x_hbm, x_ref, sems.at[0])]
    for part in range(4):
        columns = pl.ds(part % 2 * BINS + part // 2 * HALF, HALF)
        loads.append(
            pltpu.make_async_copy(table_hbm.at[:, columns], table_ref.at[:, columns], sems.at[1 + part])
        )
    loads.append(pltpu.make_async_copy(plan_hbm, plan_ref, sems.at[5]))
    loads.append(pltpu.make_async_copy(half_hbm, half_ref, sems.at[6]))
    for load in loads:
        load.start()
    residue = lax.broadcasted_iota(jnp.int32, (CH, BAND), 1) % 4
    even = residue % 2 == 0
    alternate = jnp.where(even, 1.0, -1.0)
    halfturn = jnp.where(residue < 2, 1.0, -1.0)
    loads[0].wait()
    stacked = jnp.concatenate([x_ref[0, :, r * QUART : (r + 1) * QUART] for r in range(4)], axis=0)
    reals, sines = [], []
    for half in range(2):
        loads[1 + half * 2].wait()
        low = half * HALF
        coses = jnp.dot(stacked, table_ref[:, low : low + HALF], preferred_element_type=jnp.float32)
        loads[2 + half * 2].wait()
        low += BINS
        sinuses = jnp.dot(stacked, table_ref[:, low : low + HALF], preferred_element_type=jnp.float32)
        for band in range(HALF // BAND):
            columns = slice(band * BAND, (band + 1) * BAND)
            cos = [coses[r * CH : (r + 1) * CH, columns] for r in range(4)]
            sin = [sinuses[r * CH : (r + 1) * CH, columns] for r in range(4)]
            real = cos[0] + alternate * cos[2] + halfturn * jnp.where(even, cos[1] + cos[3], sin[3] - sin[1])
            sine = sin[0] + alternate * sin[2] + halfturn * jnp.where(even, sin[1] + sin[3], cos[1] - cos[3])
            energy = jnp.mean(real * real + sine * sine, axis=1, keepdims=True)
            factor = lax.rsqrt(energy + 1e-06)
            reals.append((real * factor).astype(jnp.bfloat16).astype(jnp.float32))
            sines.append((sine * factor).astype(jnp.bfloat16).astype(jnp.float32))
    loads[5].wait()
    loads[6].wait()
    choose(plan_ref, half_ref, low_ref, high_ref, info_ref)
    rows = []
    for r in range(4):
        cos_part, sin_part = [], []
        for real, sine in zip(reals, sines):
            if r == 0:
                u, v = real, sine
            elif r == 2:
                u, v = alternate * real, alternate * sine
            else:
                turn = halfturn if r == 1 else halfturn * alternate
                u = turn * jnp.where(even, real, sine)
                v = turn * jnp.where(even, sine, -real)
            cos_part.append(u.astype(jnp.bfloat16))
            sin_part.append(v.astype(jnp.bfloat16))
        rows.append(jnp.concatenate(cos_part + sin_part, axis=1))
    turned = jnp.concatenate(rows, axis=0)
    out = lax.dot_general(
        turned, table_ref[...], (((1,), (1,)), ((), ())), preferred_element_type=jnp.float32
    ) * BINS ** (-0.5)
    series = jnp.concatenate(
        [out[r * CH : (r + 1) * CH] for r in range(4)], axis=1
    ).astype(jnp.bfloat16)
    series_ref[...] = series


def whiten(signals, table, plan, lag_half):
    smem = pl.BlockSpec(memory_space=pltpu.SMEM)
    vmem = pl.BlockSpec(memory_space=pltpu.VMEM)
    anywhere = pl.BlockSpec(memory_space=pltpu.HBM)
    return pl.pallas_call(
        whiten_kernel,
        out_shape=[
            jax.ShapeDtypeStruct((CH, NT), jnp.bfloat16),
            jax.ShapeDtypeStruct((1,), jnp.int32),
            jax.ShapeDtypeStruct((1,), jnp.int32),
            jax.ShapeDtypeStruct((8, 128), jnp.int32),
        ],
        in_specs=[anywhere] * 4,
        out_specs=[vmem, smem, smem, vmem],
        scratch_shapes=[
            pltpu.SMEM((MATCH,), jnp.int32),
            pltpu.SMEM((MATCH, 16), jnp.int32),
            pltpu.VMEM((1, CH, NT), jnp.bfloat16),
            pltpu.VMEM((QUART, NT), jnp.bfloat16),
            pltpu.SemaphoreType.DMA((7,)),
        ],
        compiler_params=pltpu.CompilerParams(vmem_limit_bytes=60 * MIB),
    )(plan, lag_half, signals, table)


def correlate_kernel(info_ref, series_ref, first_ref, second_ref, *refs, batch):
    *out_refs, fine_ref, coarse, sums, lasts = refs
    place, _ = neighbours()
    series = series_ref[...]
    for step in range(FINE):
        fine_ref[step * CH : (step + 1) * CH, :] = rolled(series, step)
    for pair, partner_ref in enumerate((first_ref, second_ref)):
        partner = partner_ref[...]
        ahead = info_ref[4 + 2 * batch + pair : 5 + 2 * batch + pair, :1] > 0
        partner = jnp.where(ahead, partner, rolled(partner, LAGS - 1))
        for step in range(COARSE + 1):
            row = (pair * (COARSE + 1) + step) * CH
            coarse[row : row + CH, :] = rolled(partner, -FINE * step)
    main = lax.dot_general(
        coarse[...], fine_ref[...], (((1,), (1,)), ((), ())), preferred_element_type=jnp.float32
    )
    for pair in range(2):
        for q in range(16):
            group = (q >> 3) * 2 + (q & 1)
            zz = (q >> 1) & 3
            for step in range(COARSE):
                row = (pair * (COARSE + 1) + step) * CH + q * 4
                sums[group, zz * 64 + pair * 32 + step * 4 : zz * 64 + pair * 32 + step * 4 + 4, :] = main[row : row + 4, :]
            for one in range(4):
                row = (pair * (COARSE + 1) + COARSE) * CH + q * 4 + one
                lasts[group, zz * 2 + pair : zz * 2 + pair + 1, one * CH : (one + 1) * CH] = main[row : row + 1, :CH]
    for r, out_ref in enumerate(out_refs):
        out_ref[0:256, :] = sums[r ^ place].astype(jnp.bfloat16)
        out_ref[256:272, :] = lasts[r ^ place].astype(jnp.bfloat16)


def correlate(info, series, first, second, batch):
    vmem = pl.BlockSpec(memory_space=pltpu.VMEM)
    return pl.pallas_call(
        functools.partial(correlate_kernel, batch=batch),
        out_shape=[jax.ShapeDtypeStruct((272, FINE * CH), jnp.bfloat16)] * 4,
        in_specs=[vmem] * 4,
        out_specs=[vmem] * 4,
        scratch_shapes=[
            pltpu.VMEM((FINE * CH, NT), jnp.bfloat16),
            pltpu.VMEM((2 * (COARSE + 1) * CH, NT), jnp.bfloat16),
            pltpu.VMEM((4, 256, FINE * CH), jnp.float32),
            pltpu.VMEM((4, 16, FINE * CH), jnp.float32),
        ],
        compiler_params=pltpu.CompilerParams(vmem_limit_bytes=24 * MIB),
        cost_estimate=pl.CostEstimate(flops=4 * CH * CH * LAGS * NT, bytes_accessed=4 << 20, transcendentals=0),
    )(info, series, first, second)


def gather_kernel(own_ref, one_ref, two_ref, three_ref, *refs):
    *out_refs, sums = refs
    _, place = neighbours()

    def total(rows):
        result = own_ref[rows, :].astype(jnp.float32)
        for other in (one_ref, two_ref, three_ref):
            result += other[rows, :].astype(jnp.float32)
        return result

    last = total(slice(256, 272))
    for zz in range(4):
        sums[zz, 0:64, :] = total(slice(zz * 64, zz * 64 + 64))
        sums[zz, 64:66, :] = last[zz * 2 : zz * 2 + 2, :]
    for r, out_ref in enumerate(out_refs):
        out_ref[...] = sums[r ^ place].astype(jnp.bfloat16)


def gather(terms):
    vmem = pl.BlockSpec(memory_space=pltpu.VMEM)
    return pl.pallas_call(
        gather_kernel,
        out_shape=[jax.ShapeDtypeStruct((80, FINE * CH), jnp.bfloat16)] * 4,
        in_specs=[vmem] * 4,
        out_specs=[vmem] * 4,
        scratch_shapes=[pltpu.VMEM((4, 80, FINE * CH), jnp.float32)],
        compiler_params=pltpu.CompilerParams(vmem_limit_bytes=16 * MIB),
    )(*terms)


def finish_kernel(info_ref, *refs, factor):
    out_ref = refs[8]
    width = 4 * LAGS
    rows = lax.broadcasted_iota(jnp.int32, (132, width), 0)
    columns = lax.broadcasted_iota(jnp.int32, (132, width), 1)
    lag = jnp.where(rows < 128, (rows % 32) // 4 * FINE + rows // 32, LAGS - 1)
    ahead = (columns == rows % 4 * LAGS + lag).astype(jnp.float32)
    behind = (columns == rows % 4 * LAGS + LAGS - 1 - lag).astype(jnp.float32)
    for batch in range(2):
        own_ref, *others = refs[batch * 4 : batch * 4 + 4]
        total = own_ref[:66, :].astype(jnp.float32)
        for other in others:
            total += other[:66, :].astype(jnp.float32)
        total *= factor
        for pair in range(2):
            slot = batch * 2 + pair
            pick = jnp.where(info_ref[4 + slot : 5 + slot, :1] > 0, ahead, behind).astype(jnp.bfloat16)
            pieces = [total[pair * 32 : pair * 32 + 32, k * CH : (k + 1) * CH] for k in range(FINE)]
            pieces += [total[64 + pair : 65 + pair, k * CH : (k + 1) * CH] for k in range(FINE)]
            stacked = jnp.concatenate(pieces, axis=0).T
            top = stacked.astype(jnp.bfloat16)
            rest = (stacked - top.astype(jnp.float32)).astype(jnp.bfloat16)
            result = jnp.dot(top, pick, preferred_element_type=jnp.float32)
            result += jnp.dot(rest, pick, preferred_element_type=jnp.float32)
            out_ref[jnp.max(info_ref[slot : slot + 1, :])] = result


def finish(info, terms, factor):
    vmem = pl.BlockSpec(memory_space=pltpu.VMEM)
    return pl.pallas_call(
        functools.partial(finish_kernel, factor=factor),
        out_shape=jax.ShapeDtypeStruct((MATCH, CH, 4 * LAGS), jnp.float32),
        in_specs=[vmem] * 9,
        out_specs=vmem,
        compiler_params=pltpu.CompilerParams(vmem_limit_bytes=16 * MIB),
    )(info, *terms)


def exchange(series, mask):
    return lax.ppermute(series, "chan", [(block, block ^ mask) for block in range(16)])


def pass_on(block, mask):
    return lax.ppermute(block, "win", [(window, window ^ mask) for window in range(16)])


def to_neighbours(terms):
    return [terms[0]] + [pass_on(terms[d], (d >> 1) * 8 + (d & 1)) for d in (2, 1, 3)]


def along_z(sums):
    return [sums[0]] + [pass_on(sums[d], 2 * d) for d in (1, 2, 3)]


def shards(signals, plan, lag_half):
    table = jnp.asarray(quarter_table())
    series, first, second, info = whiten(signals, table, plan, lag_half)
    branches = [lambda s, a=a: exchange(s, a) for a in range(2, 15)]
    near = exchange(series, 1)
    low = lax.switch(first.reshape(()), branches, series)
    later, low = lax.optimization_barrier((series, low))
    far = exchange(later, 15)
    terms = correlate(info, series, near, low, 0)
    later, terms = lax.optimization_barrier((series, terms))
    high = lax.switch(second.reshape(()), branches, later)
    terms, high = lax.optimization_barrier((to_neighbours(terms), high))
    sums = gather(terms)
    far, high, sums = lax.optimization_barrier((far, high, sums))
    last_sums = gather(to_neighbours(correlate(info, series, far, high, 1)))
    return finish(info, along_z(sums) + along_z(last_sums), 1.0 / math.sqrt(lax.axis_size("win") * NT))


def solution(mesh):
    placed = (P("win", "chan", None), P(), P())
    return jax.shard_map(
        shards, mesh=mesh, in_specs=placed, out_specs=P(None, "chan", "win"), check_vma=False
    )
```
